32 devices in a mesh: slab: 2 (over y), row: 8 (over z, x), sub: 2 (over core).
Axes of the slice: x: 2, y: 2, z: 4, core: 2. Of those that a mesh axis runs over, the one named last changes fastest.
Arguments:
- states: bfloat16 [8192, 1024], P(('slab', 'row'), 'sub'), parts along dimension 0, may hold values from -6 to 6
- rotation: bfloat16 [1024, 1024], P(None, 'sub'), may hold values from -0.1875 to 0.1875
- codes: int32 [8192, 64], P(('slab', 'row'), 'sub'), parts along dimension 0, may hold values from 0 to 255
- prior_codebook: float32 [128, 256, 16], P(('slab', 'sub')), parts along dimension 0, may hold values from -6 to 6
Outputs:
- codebook: float32 [128, 256, 16], P(('slab', 'sub')), parts along dimension 0
- cross: float32 [2048, 1024], P(('slab', 'row'), 'sub'), parts along dimension 0
The draws below stay inside these ranges and needn't reach their ends.
There are 2 independent parts, one for each index of `slab`. The reference program is written for one: setup_inputs(seed, part) draws one part's arguments, and reference() takes and returns one part's arrays. A program takes and returns all parts, laid end to end along the dimension named above; an argument that names none is the same for every part. Nothing has to cross between parts.
All inputs are finite; a program needn't handle non-finite values.
Results may differ from the reference program's by a relative error of at most 0.0036.
Values may be sent and summed in bfloat16 or wider, within the bound.
A program may use at most 64 MiB of HBM per device.

```python
import math
import jax
import jax.numpy as jnp
import numpy as np
from jax import lax

D = 1024
SUBDIM = 16
K = 256
SUBS = 64
ROWS = 4096


def place_ends(array, own_key, smallest, top_value):
    extent = array.shape
    index_at = [jax.random.randint(jax.random.fold_in(own_key, axis), (), 0, extent[axis]) for axis in range(len(extent))]
    array = array.at[tuple(index_at)].set(smallest)
    longest = extent.index(max(extent))
    index_at[longest] = (index_at[longest] + 1) % extent[longest]
    return array.at[tuple(index_at)].set(top_value)


def raised(drawn, key, source, target, shards_of, factor):
    owner, partner = [(jnp.arange(drawn.shape[position]) // (drawn.shape[position] // shards_of)).reshape([-1 if axis == position else 1 for axis in range(drawn.ndim)]) for position in (source, target)]
    chosen = jax.random.permutation(key, shards_of)[partner]
    strong = (owner == chosen) | (owner == (partner + shards_of // 2) % shards_of)
    return jnp.where(strong, factor * drawn, drawn)


def steps_of(stream_key, shape, shards, least, top_value):
    def one(axis_at, shards_of):
        heights = jax.random.uniform(jax.random.fold_in(jax.random.fold_in(stream_key, 6), axis_at), (shards_of,), jnp.float32, least / len(shards), top_value / len(shards))
        return jnp.repeat(jnp.exp(heights), shape[axis_at] // shards_of).reshape((-1,) + (1,) * (len(shape) - axis_at - 1))

    factor_of = one(*shards[0])
    for cut in shards[1:]:
        factor_of = factor_of * one(*cut)
    return factor_of


def rank_bounds(number_of, skew):
    portions = [(1 << 20) // math.isqrt(standing ** skew) + 1 for standing in range(1, number_of + 1)]
    scale = 1 + sum(portions) // (1 << 30)
    return np.cumsum(np.array([max(1, weight // scale) for weight in portions]))


def ranked_ids(rng, dims, number_of, lean):
    grid = rank_bounds(number_of, lean)
    lot = jax.random.randint(jax.random.fold_in(rng, 1), dims, 0, int(grid[number_of - 1]))
    grade = jnp.searchsorted(jnp.asarray(grid, jnp.int32), lot, side="right")
    return jax.random.permutation(jax.random.fold_in(rng, 2), number_of)[grade].astype(jnp.int32)


def bell_draw(rng, shape, width, limit, pieces=(), kind=jnp.bfloat16):
    result = jax.random.normal(rng, shape, jnp.float32) * width
    if len(pieces) > 0:
        result = steps_of(rng, shape, pieces, -0.22, 0.18) * result
    return jnp.clip(result, min=-limit, max=limit).astype(kind)


def heavy_noise(own_key, shape, scale, reach, cuts, heavy, kind=jnp.bfloat16):
    drawn = scale * jax.random.normal(own_key, shape, jnp.float32)
    if cuts:
        drawn = drawn * steps_of(own_key, shape, cuts, -0.22, 0.18)
    return jnp.clip(raised(drawn, jax.random.fold_in(own_key, 3), *heavy), -reach, reach).astype(kind)


def setup_inputs(seed: int = 0, part: int = 0) -> dict:
    key_of = jax.random.split(jax.random.key(seed), 5)
    own_keys = jax.random.split(jax.random.fold_in(key_of[4], part), 5)
    return {
        "states": heavy_noise(own_keys[0], (ROWS, D), 1.0, 6.0, ((0, 8), (1, 2)), (0, 1, 8, 2.0)),
        "rotation": bell_draw(key_of[1], (D, D), D ** -0.5, 0.1875, ((1, 2),)),
        "codes": place_ends(ranked_ids(own_keys[2], (ROWS, SUBS), K, 2), jax.random.fold_in(own_keys[2], 3), 0, K - 1).astype(jnp.int32),
        "prior_codebook": bell_draw(own_keys[3], (SUBS, K, SUBDIM), 1.0, 6.0, ((0, 2),), jnp.float32),
    }


def reference(states, rotation, codes, prior_codebook):
    rotated = jnp.dot(states, rotation, preferred_element_type=jnp.float32).astype(jnp.bfloat16)

    def fit_one(index):
        block = lax.dynamic_slice_in_dim(rotated, index * SUBDIM, SUBDIM, 1).astype(jnp.float32)
        column = lax.dynamic_slice_in_dim(codes, index, 1, 1)[:, 0]
        sums = jax.ops.segment_sum(block, column, num_segments=K)
        counts = jax.ops.segment_sum(jnp.ones((ROWS,), jnp.float32), column, num_segments=K)
        return sums, counts

    sums, counts = lax.map(fit_one, jnp.arange(SUBS, dtype=jnp.int32))
    codebook = (sums + prior_codebook) / (counts[:, :, None] + 1.0)
    small_book = codebook.astype(jnp.bfloat16)
    rebuilt = small_book[jnp.arange(SUBS)[None, :], codes].reshape(ROWS, D)
    cross = lax.dot_general(states, rebuilt, (((0,), (0,)), ((), ())), preferred_element_type=jnp.float32)
    return codebook, cross
```

```python
import functools
import math

import jax
import jax.numpy as jnp
from jax import lax
from jax.experimental import pallas as pl
from jax.experimental.pallas import tpu as pltpu
from jax.sharding import PartitionSpec as P

SUBDIM = 16
K = 256


def shards(states, rotation, codes, prior_codebook):
    row_keys = states.shape[0]
    local_subs = codes.shape[1]
    local_width = rotation.shape[1]
    rows_count = lax.axis_size("row")
    labels = jnp.arange(K, dtype=jnp.int32)
    full_states = lax.all_gather(states, "sub", axis=1, tiled=True)
    rotated = jnp.dot(full_states, rotation, preferred_element_type=jnp.float32).astype(
        jnp.bfloat16
    )
    owned = local_width // rows_count
    repeat = max(1, SUBDIM // owned)
    owned_codes = max(1, owned // SUBDIM)
    piece_width = owned // owned_codes
    spread_codes = jnp.repeat(codes, repeat, axis=1)
    moved_rows, moved_codes = (
        lax.all_to_all(rotated, "row", split_axis=1, concat_axis=0, tiled=True),
        lax.all_to_all(spread_codes, "row", split_axis=1, concat_axis=0, tiled=True),
    )
    all_keys = moved_rows.shape[0]
    block_rows = math.gcd(all_keys, 4096)
    block_count = all_keys // block_rows
    rows_blocks = moved_rows.reshape(block_count, block_rows, owned)
    codes_blocks = moved_codes.reshape(block_count, block_rows, moved_codes.shape[1])

    def add_block(carry, pair):
        total_sum, total_count = carry
        row_block, code_block = pair
        new_sums = []
        new_counts = []
        for which in range(owned_codes):
            onehot = (code_block[:, which][:, None] == labels[None, :]).astype(jnp.bfloat16)
            piece = row_block[:, which * piece_width : (which + 1) * piece_width]
            new_sums.append(
                lax.dot_general(
                    onehot, piece, (((0,), (0,)), ((), ())), preferred_element_type=jnp.float32
                )
            )
            new_counts.append(jnp.sum(onehot, axis=0, dtype=jnp.float32))
        return ((total_sum + jnp.stack(new_sums), total_count + jnp.stack(new_counts)), None)

    start_sum = jnp.zeros((owned_codes, K, piece_width), jnp.float32)
    start_count = jnp.zeros((owned_codes, K), jnp.float32)
    (owner_sum, owner_count), _ = lax.scan(
        add_block, (start_sum, start_count), (rows_blocks, codes_blocks)
    )
    every_sum, every_count = (
        lax.all_gather(owner_sum, "row", axis=0, tiled=True),
        lax.all_gather(owner_count, "row", axis=0, tiled=True),
    )
    pieces = SUBDIM // piece_width
    sums = (
        every_sum.reshape(local_subs, pieces, K, piece_width)
        .transpose(0, 2, 1, 3)
        .reshape(local_subs, K, SUBDIM)
    )
    counts = every_count.reshape(local_subs, pieces, K)[:, 0, :]
    codebook = (sums + prior_codebook) / (counts[:, :, None] + 1.0)
    small_book = codebook.astype(jnp.bfloat16)
    group_size = math.gcd(8, local_subs)
    group_count = local_subs // group_size
    book_groups = small_book.reshape(group_count, group_size, K, SUBDIM)
    code_groups = codes.T.reshape(group_count, group_size, row_keys)

    def lookup_group(pair):
        book_part, code_part = pair
        onehot = (code_part[:, :, None] == labels[None, None, :]).astype(jnp.bfloat16)
        found = lax.dot_general(
            onehot, book_part, (((2,), (1,)), ((0,), (0,))), preferred_element_type=jnp.float32
        )
        return found.astype(jnp.bfloat16)

    looked = lax.map(lookup_group, (book_groups, code_groups))
    rebuilt = (
        looked.reshape(local_subs, row_keys, SUBDIM)
        .transpose(1, 0, 2)
        .reshape(row_keys, local_width)
    )
    cross = lax.psum_scatter(
        lax.dot_general(
            full_states, rebuilt, (((0,), (0,)), ((), ())), preferred_element_type=jnp.float32
        ),
        "row",
        scatter_dimension=0,
        tiled=True,
    )
    return (codebook, cross)


MESH = pl.DeviceIdType.MESH
BF16 = jnp.bfloat16
F32 = jnp.float32
NT = (((1,), (1,)), ((), ()))


def kernel(
    rows_count,
    states_ref,
    rotation_ref,
    codes_ref,
    prior_ref,
    book_ref,
    cross_ref,
    other,
    states_t,
    rotated_t,
    onehot,
    part,
    pair_sum,
    line_out,
    line_sum,
    small_book,
    rebuilt_t,
    cross_out,
    cross_keep,
    cross_pair,
    cross_line_out,
    cross_line,
    send_sem,
    recv_sem,
):
    outer = rows_count // 2
    me = lax.axis_index("row")
    sub = lax.axis_index("sub")
    deep, side = me // 2, me % 2
    mate = deep * 2 + 1 - side
    half = states_ref.shape[1]
    subs = codes_ref.shape[0]
    owned = subs // rows_count
    feats = owned * SUBDIM
    block = cross_ref.shape[0]
    hops = sorted(range(outer), key=lambda k: (k == 0, -min(k, outer - k)))
    used = []

    def copy(src, dst, where):
        index = len(used)
        made = pltpu.make_async_remote_copy(
            src_ref=src,
            dst_ref=dst,
            send_sem=send_sem.at[index],
            recv_sem=recv_sem.at[index],
            device_id=where,
            device_id_type=MESH,
        )
        made.start()
        used.append(made)
        return made

    def line(k):
        return lax.rem(deep + k, outer)

    barrier = pltpu.get_barrier_semaphore()
    pl.semaphore_signal(barrier, inc=1, device_id={"sub": 1 - sub}, device_id_type=MESH)
    pl.semaphore_signal(barrier, inc=1, device_id={"row": mate}, device_id_type=MESH)
    for k in range(1, outer):
        pl.semaphore_signal(
            barrier, inc=1, device_id={"row": line(k) * 2 + side}, device_id_type=MESH
        )
    pl.semaphore_wait(barrier, outer + 1)

    swap = copy(states_ref, other, {"sub": 1 - sub})
    total = jnp.dot(
        states_ref[...],
        rotation_ref[pl.ds(pl.multiple_of(sub * half, half), half), :],
        preferred_element_type=F32,
    )
    swap.wait_recv()
    total = total + jnp.dot(
        other[...],
        rotation_ref[pl.ds(pl.multiple_of((1 - sub) * half, half), half), :],
        preferred_element_type=F32,
    )
    rotated_t[...] = total.astype(BF16).T

    keys = states_ref.shape[0]
    labels = lax.broadcasted_iota(jnp.int32, (K, keys), 0)
    ones = jnp.ones((SUBDIM, keys), BF16)

    def sum_block(owner):
        for j in range(owned):
            m = owner * owned + j
            row = codes_ref[pl.ds(m, 1), :]
            hot = jnp.where(row == labels, 1.0, 0.0).astype(BF16)
            onehot[m] = hot
            piece = rotated_t[pl.ds(pl.multiple_of(m * SUBDIM, SUBDIM), SUBDIM), :]
            found = lax.dot_general(
                jnp.concatenate([piece, ones], axis=0), hot, NT, preferred_element_type=F32
            )
            part[owner, j * SUBDIM : (j + 1) * SUBDIM, :] = found[:SUBDIM]
            part[owner, feats + 2 * j : feats + 2 * j + 2, :] = found[SUBDIM : SUBDIM + 2]

    pair = {}
    for k in hops:
        owner = line(k) * 2 + 1 - side
        sum_block(owner)
        pair[k] = copy(part.at[owner], pair_sum.at[k], {"row": mate})
    for k in hops:
        sum_block(line(k) * 2 + side)
    lines = {}
    mine = None
    for k in hops:
        pair[k].wait_recv()
        both = part[line(k) * 2 + side] + pair_sum[k]
        if k == 0:
            mine = both
        else:
            line_out[k - 1] = both
            lines[k] = copy(
                line_out.at[k - 1], line_sum.at[k - 1], {"row": line(k) * 2 + side}
            )

    states_t[pl.ds(pl.multiple_of(sub * half, half), half), :] = states_ref[...].T
    states_t[pl.ds(pl.multiple_of((1 - sub) * half, half), half), :] = other[...].T

    for k in hops:
        if k != 0:
            lines[k].wait_recv()
            mine = mine + line_sum[k - 1]
    for j in range(owned):
        own_rows = pl.ds(pl.multiple_of(me * feats, feats) + j * SUBDIM, SUBDIM)
        fitted = (mine[j * SUBDIM : (j + 1) * SUBDIM] + prior_ref[own_rows, :]) / (
            mine[feats + 2 * j : feats + 2 * j + 1] + 1.0
        )
        small_book[own_rows, :] = fitted.astype(BF16)

    def book_rows(owner):
        return small_book.at[pl.ds(pl.multiple_of(owner * feats, feats), feats), :]

    along = {}
    for k in hops:
        if k != 0:
            along[k] = copy(book_rows(me), book_rows(me), {"row": line(k) * 2 + side})
    across = {0: copy(book_rows(me), book_rows(me), {"row": mate})}

    def look_up(owner):
        for j in range(owned):
            m = owner * owned + j
            rows = pl.ds(pl.multiple_of(m * SUBDIM, SUBDIM), SUBDIM)
            book = small_book[rows, :]
            book_ref[rows, :] = book.astype(F32)
            rebuilt_t[rows, :] = jnp.dot(
                book, onehot[m], preferred_element_type=F32
            ).astype(BF16)

    look_up(me)
    order = [k for k in reversed(hops) if k != 0]
    for k in order:
        along[k].wait_recv()
        source = lax.rem(deep + outer - k, outer) * 2 + side
        across[k] = copy(book_rows(source), book_rows(source), {"row": mate})
        look_up(source)
    across[0].wait_recv()
    look_up(mate)
    for k in order:
        across[k].wait_recv()
        look_up(lax.rem(deep + outer - k, outer) * 2 + 1 - side)

    def cross_block(owner):
        rows = pl.ds(pl.multiple_of(owner * block, block), block)
        return lax.dot_general(
            states_t[rows, :], rebuilt_t[...], NT, preferred_element_type=F32
        )

    for k in hops:
        cross_out[k] = cross_block(line(k) * 2 + 1 - side).astype(BF16)
        pair[k] = copy(cross_out.at[k], cross_pair.at[k], {"row": mate})
    for k in hops:
        cross_keep[k] = cross_block(line(k) * 2 + side)
    for k in hops:
        pair[k].wait_recv()
        both = cross_keep[k] + cross_pair[k].astype(F32)
        if k == 0:
            cross_ref[...] = both
        else:
            cross_line_out[k - 1] = both.astype(BF16)
            lines[k] = copy(
                cross_line_out.at[k - 1], cross_line.at[k - 1], {"row": line(k) * 2 + side}
            )
    for k in order:
        lines[k].wait_recv()
        cross_ref[...] += cross_line[k - 1].astype(F32)
    for made in used:
        made.wait_send()


def fused(rows_count, states, rotation, codes, prior_codebook):
    keys, half = states.shape
    width = rotation.shape[1]
    subs = codes.shape[1]
    outer = rows_count // 2
    feats = subs // rows_count * SUBDIM
    tall = feats + 2 * (subs // rows_count)
    block = rotation.shape[0] // rows_count
    copies = 5 * outer + 1 + 3 * (outer - 1) + 8
    vmem = pl.BlockSpec(memory_space=pltpu.VMEM)
    book_t, cross = pl.pallas_call(
        functools.partial(kernel, rows_count),
        out_shape=(
            jax.ShapeDtypeStruct((subs * SUBDIM, K), F32),
            jax.ShapeDtypeStruct((block, width), F32),
        ),
        in_specs=[vmem] * 4,
        out_specs=(vmem, vmem),
        scratch_shapes=[
            pltpu.VMEM((keys, half), BF16),
            pltpu.VMEM((2 * half, keys), BF16),
            pltpu.VMEM((width, keys), BF16),
            pltpu.VMEM((subs, K, keys), BF16),
            pltpu.VMEM((rows_count, tall, K), F32),
            pltpu.VMEM((outer, tall, K), F32),
            pltpu.VMEM((outer - 1, tall, K), F32),
            pltpu.VMEM((outer - 1, tall, K), F32),
            pltpu.VMEM((width, K), BF16),
            pltpu.VMEM((width, keys), BF16),
            pltpu.VMEM((outer, block, width), BF16),
            pltpu.VMEM((outer, block, width), F32),
            pltpu.VMEM((outer, block, width), BF16),
            pltpu.VMEM((outer - 1, block, width), BF16),
            pltpu.VMEM((outer - 1, block, width), BF16),
            pltpu.SemaphoreType.DMA((copies,)),
            pltpu.SemaphoreType.DMA((copies,)),
        ],
        compiler_params=pltpu.CompilerParams(
            collective_id=0, has_side_effects=True, vmem_limit_bytes=48 * 1024 * 1024
        ),
    )(
        states,
        rotation,
        codes.T,
        prior_codebook.transpose(0, 2, 1).reshape(subs * SUBDIM, K),
    )
    return book_t.reshape(subs, SUBDIM, K).transpose(0, 2, 1), cross


def pick(mesh):
    rows_count = mesh.shape["row"]

    def run(states, rotation, codes, prior_codebook):
        fits = (
            rows_count % 2 == 0
            and rows_count <= 16
            and codes.shape[1] % rows_count == 0
            and (codes.shape[1] // rows_count * 2) % 8 == 0
            and rotation.shape[0] % (16 * rows_count) == 0
        )
        if not fits:
            return shards(states, rotation, codes, prior_codebook)
        return fused(rows_count, states, rotation, codes, prior_codebook)

    return run


def solution(mesh):
    placed = (
        P(("slab", "row"), "sub"),
        P(None, "sub"),
        P(("slab", "row"), "sub"),
        P(("slab", "sub"), None, None),
    )
    return jax.shard_map(
        pick(mesh),
        mesh=mesh,
        in_specs=placed,
        out_specs=(P(("slab", "sub"), None, None), P(("slab", "row"), "sub")),
        check_vma=False,
    )
```

```python
import functools
import math

import jax
import jax.numpy as jnp
from jax import lax
from jax.experimental import pallas as pl
from jax.experimental.pallas import tpu as pltpu
from jax.sharding import PartitionSpec as P

SUBDIM = 16
K = 256


def shards(states, rotation, codes, prior_codebook):
    row_keys = states.shape[0]
    local_subs = codes.shape[1]
    local_width = rotation.shape[1]
    rows_count = lax.axis_size("row")
    labels = jnp.arange(K, dtype=jnp.int32)
    full_states = lax.all_gather(states, "sub", axis=1, tiled=True)
    rotated = jnp.dot(full_states, rotation, preferred_element_type=jnp.float32).astype(
        jnp.bfloat16
    )
    owned = local_width // rows_count
    repeat = max(1, SUBDIM // owned)
    owned_codes = max(1, owned // SUBDIM)
    piece_width = owned // owned_codes
    spread_codes = jnp.repeat(codes, repeat, axis=1)
    moved_rows, moved_codes = (
        lax.all_to_all(rotated, "row", split_axis=1, concat_axis=0, tiled=True),
        lax.all_to_all(spread_codes, "row", split_axis=1, concat_axis=0, tiled=True),
    )
    all_keys = moved_rows.shape[0]
    block_rows = math.gcd(all_keys, 4096)
    block_count = all_keys // block_rows
    rows_blocks = moved_rows.reshape(block_count, block_rows, owned)
    codes_blocks = moved_codes.reshape(block_count, block_rows, moved_codes.shape[1])

    def add_block(carry, pair):
        total_sum, total_count = carry
        row_block, code_block = pair
        new_sums = []
        new_counts = []
        for which in range(owned_codes):
            onehot = (code_block[:, which][:, None] == labels[None, :]).astype(jnp.bfloat16)
            piece = row_block[:, which * piece_width : (which + 1) * piece_width]
            new_sums.append(
                lax.dot_general(
                    onehot, piece, (((0,), (0,)), ((), ())), preferred_element_type=jnp.float32
                )
            )
            new_counts.append(jnp.sum(onehot, axis=0, dtype=jnp.float32))
        return ((total_sum + jnp.stack(new_sums), total_count + jnp.stack(new_counts)), None)

    start_sum = jnp.zeros((owned_codes, K, piece_width), jnp.float32)
    start_count = jnp.zeros((owned_codes, K), jnp.float32)
    (owner_sum, owner_count), _ = lax.scan(
        add_block, (start_sum, start_count), (rows_blocks, codes_blocks)
    )
    every_sum, every_count = (
        lax.all_gather(owner_sum, "row", axis=0, tiled=True),
        lax.all_gather(owner_count, "row", axis=0, tiled=True),
    )
    pieces = SUBDIM // piece_width
    sums = (
        every_sum.reshape(local_subs, pieces, K, piece_width)
        .transpose(0, 2, 1, 3)
        .reshape(local_subs, K, SUBDIM)
    )
    counts = every_count.reshape(local_subs, pieces, K)[:, 0, :]
    codebook = (sums + prior_codebook) / (counts[:, :, None] + 1.0)
    small_book = codebook.astype(jnp.bfloat16)
    group_size = math.gcd(8, local_subs)
    group_count = local_subs // group_size
    book_groups = small_book.reshape(group_count, group_size, K, SUBDIM)
    code_groups = codes.T.reshape(group_count, group_size, row_keys)

    def lookup_group(pair):
        book_part, code_part = pair
        onehot = (code_part[:, :, None] == labels[None, None, :]).astype(jnp.bfloat16)
        found = lax.dot_general(
            onehot, book_part, (((2,), (1,)), ((0,), (0,))), preferred_element_type=jnp.float32
        )
        return found.astype(jnp.bfloat16)

    looked = lax.map(lookup_group, (book_groups, code_groups))
    rebuilt = (
        looked.reshape(local_subs, row_keys, SUBDIM)
        .transpose(1, 0, 2)
        .reshape(row_keys, local_width)
    )
    cross = lax.psum_scatter(
        lax.dot_general(
            full_states, rebuilt, (((0,), (0,)), ((), ())), preferred_element_type=jnp.float32
        ),
        "row",
        scatter_dimension=0,
        tiled=True,
    )
    return (codebook, cross)


MESH = pl.DeviceIdType.MESH
BF16 = jnp.bfloat16
F32 = jnp.float32
NT = (((1,), (1,)), ((), ()))


def kernel(
    rows_count,
    states_ref,
    rotation_ref,
    codes_ref,
    prior_ref,
    book_ref,
    cross_ref,
    states_v,
    rotation_v,
    codes_v,
    prior_v,
    other,
    all_states,
    all_codes,
    codes_i,
    rotated_t,
    part,
    pair_sum,
    line_out,
    line_sum,
    small_book,
    rebuilt_t,
    local_sem,
    send_sem,
    recv_sem,
    out_sem,
    pass_sem,
    block_sem,
):
    outer = rows_count // 2
    me = lax.axis_index("row")
    sub = lax.axis_index("sub")
    deep, side = me // 2, me % 2
    mate = deep * 2 + 1 - side
    keys, half = states_v.shape
    subs = codes_v.shape[0]
    owned = subs // rows_count
    feats = owned * SUBDIM
    block = cross_ref.shape[0]
    per_half = rows_count // 2
    primary = me // per_half == sub
    hops = sorted(range(outer), key=lambda k: (k == 0, -min(k, outer - k)))
    order = [k for k in reversed(hops) if k != 0]
    used = []

    def copy(src, dst, where):
        index = len(used)
        made = pltpu.make_async_remote_copy(
            src_ref=src,
            dst_ref=dst,
            send_sem=send_sem.at[index],
            recv_sem=recv_sem.at[index],
            device_id=where,
            device_id_type=MESH,
        )
        made.start()
        used.append(made)
        return made

    def line(k):
        return lax.rem(deep + k, outer)

    def back(k):
        return lax.rem(deep + outer - k, outer)

    loads = []
    for index, (src, dst) in enumerate(
        (
            (states_ref, states_v),
            (codes_ref, codes_v),
            (rotation_ref, rotation_v),
            (prior_ref, prior_v),
        )
    ):
        loads.append(pltpu.make_async_copy(src, dst, local_sem.at[index]))
        loads[-1].start()

    barrier = pltpu.get_barrier_semaphore()
    pl.semaphore_signal(barrier, inc=1, device_id={"sub": 1 - sub}, device_id_type=MESH)
    for k in range(1, rows_count):
        pl.semaphore_signal(
            barrier, inc=1, device_id={"row": lax.rem(me + k, rows_count)}, device_id_type=MESH
        )
    pl.semaphore_wait(barrier, rows_count)

    loads[0].wait()
    swap = copy(states_v, other, {"sub": 1 - sub})

    def columns(q):
        return states_v.at[:, pl.ds(pl.multiple_of(q * block, block), block)]

    def give(q):
        owner = sub * per_half + q
        return pltpu.make_async_remote_copy(
            src_ref=columns(q),
            dst_ref=all_states.at[me],
            send_sem=out_sem.at[q],
            recv_sem=block_sem.at[me],
            device_id={"row": owner},
            device_id_type=MESH,
        )

    def forward(source):
        return pltpu.make_async_remote_copy(
            src_ref=all_states.at[source],
            dst_ref=all_states.at[source],
            send_sem=pass_sem.at[source],
            recv_sem=block_sem.at[source],
            device_id={"sub": 1 - sub},
            device_id_type=MESH,
        )

    loads[1].wait()
    all_codes[me] = codes_v[...].astype(F32).astype(BF16)
    codes_along = {}
    for k in hops:
        if k != 0:
            codes_along[k] = copy(
                all_codes.at[me], all_codes.at[me], {"row": line(k) * 2 + side}
            )
    codes_across = {0: copy(all_codes.at[me], all_codes.at[me], {"row": mate})}
    for q in range(per_half):

        @pl.when(sub * per_half + q != me)
        def _():
            give(q).start()

    @pl.when(primary)
    def _():
        all_states[me] = columns(lax.rem(me, per_half))[...]
        forward(me).start()

    loads[2].wait()
    total = jnp.dot(
        states_v[...],
        rotation_v[pl.ds(pl.multiple_of(sub * half, half), half), :],
        preferred_element_type=F32,
    )
    swap.wait_recv()
    total = total + jnp.dot(
        other[...],
        rotation_v[pl.ds(pl.multiple_of((1 - sub) * half, half), half), :],
        preferred_element_type=F32,
    )
    rotated_t[...] = total.astype(BF16).T

    labels = lax.broadcasted_iota(jnp.int32, (K, keys), 0)
    ones = jnp.ones((SUBDIM, keys), BF16)

    def sum_block(owner):
        for j in range(owned):
            m = owner * owned + j
            row = codes_v[pl.ds(m, 1), :]
            hot = jnp.where(row == labels, 1.0, 0.0).astype(BF16)
            piece = rotated_t[pl.ds(pl.multiple_of(m * SUBDIM, SUBDIM), SUBDIM), :]
            found = lax.dot_general(
                jnp.concatenate([piece, ones], axis=0), hot, NT, preferred_element_type=F32
            )
            part[owner, j * SUBDIM : (j + 1) * SUBDIM, :] = found[:SUBDIM]
            part[owner, feats + 2 * j : feats + 2 * j + 2, :] = found[SUBDIM : SUBDIM + 2]

    pair = {}
    for k in hops:
        owner = line(k) * 2 + 1 - side
        sum_block(owner)
        pair[k] = copy(part.at[owner], pair_sum.at[k], {"row": mate})
    for k in hops:
        sum_block(line(k) * 2 + side)
    lines = {}
    mine = None
    for k in hops:
        pair[k].wait_recv()
        both = part[line(k) * 2 + side] + pair_sum[k]
        if k == 0:
            mine = both
        else:
            line_out[k - 1] = both
            lines[k] = copy(
                line_out.at[k - 1], line_sum.at[k - 1], {"row": line(k) * 2 + side}
            )
    for k in order:
        codes_along[k].wait_recv()
        source = back(k) * 2 + side
        codes_across[k] = copy(all_codes.at[source], all_codes.at[source], {"row": mate})
    loads[3].wait()
    for k in hops:
        if k != 0:
            lines[k].wait_recv()
            mine = mine + line_sum[k - 1]
    for j in range(owned):
        own_rows = pl.ds(pl.multiple_of(me * feats, feats) + j * SUBDIM, SUBDIM)
        fitted = (mine[j * SUBDIM : (j + 1) * SUBDIM] + prior_v[own_rows, :]) / (
            mine[feats + 2 * j : feats + 2 * j + 1] + 1.0
        )
        small_book[own_rows, :] = fitted.astype(BF16)

    def book_rows(owner):
        return small_book.at[pl.ds(pl.multiple_of(owner * feats, feats), feats), :]

    along = {}
    for k in hops:
        if k != 0:
            along[k] = copy(book_rows(me), book_rows(me), {"row": line(k) * 2 + side})
    across = {0: copy(book_rows(me), book_rows(me), {"row": mate})}

    for k in range(1, rows_count):
        source = lax.rem(me + k, rows_count)
        forward(source).wait_recv()

        @pl.when(primary)
        def _():
            forward(source).start()

    for k in order:
        codes_across[k].wait_recv()
    codes_across[0].wait_recv()

    def look_up(owner):
        for j in range(owned):
            m = owner * owned + j
            rows = pl.ds(pl.multiple_of(m * SUBDIM, SUBDIM), SUBDIM)
            book_ref[rows, :] = small_book[rows, :].astype(F32)

        @pl.loop(0, rows_count)
        def _(source):
            base = pl.multiple_of(owner * owned, owned)
            for j in range(owned):
                rows = pl.ds(pl.multiple_of((base + j) * SUBDIM, SUBDIM), SUBDIM)
                row = all_codes_f(source, base, j)
                hot = jnp.where(row == labels, 1.0, 0.0).astype(BF16)
                rebuilt_t[source, rows, :] = jnp.dot(
                    small_book[rows, :], hot, preferred_element_type=F32
                ).astype(BF16)

    def all_codes_f(source, base, j):
        return codes_i[source, pl.ds(base + j, 1), :]

    for source in range(rows_count):
        codes_i[source] = all_codes[source].astype(F32).astype(jnp.int32)
    look_up(me)
    for k in order:
        along[k].wait_recv()
        source = back(k) * 2 + side
        across[k] = copy(book_rows(source), book_rows(source), {"row": mate})
    for k in order:
        look_up(back(k) * 2 + side)
    across[0].wait_recv()
    look_up(mate)
    for k in order:
        across[k].wait_recv()
        look_up(back(k) * 2 + 1 - side)

    @pl.when(jnp.logical_not(primary))
    def _():
        forward(me).wait_recv()

    total = jnp.zeros(cross_ref.shape, F32)
    for source in range(rows_count):
        total = total + lax.dot_general(
            all_states[source].T, rebuilt_t[source], NT, preferred_element_type=F32
        )
    cross_ref[...] = total

    for q in range(per_half):

        @pl.when(sub * per_half + q != me)
        def _():
            give(q).wait_send()

    @pl.when(primary)
    def _():
        for source in range(rows_count):
            forward(source).wait_send()

    for made in used:
        made.wait_send()


def fused(rows_count, states, rotation, codes, prior_codebook):
    keys, half = states.shape
    width = rotation.shape[1]
    subs = codes.shape[1]
    outer = rows_count // 2
    feats = subs // rows_count * SUBDIM
    tall = feats + 2 * (subs // rows_count)
    block = rotation.shape[0] // rows_count
    copies = 7 * outer
    vmem = pl.BlockSpec(memory_space=pltpu.VMEM)
    book_t, cross = pl.pallas_call(
        functools.partial(kernel, rows_count),
        out_shape=(
            jax.ShapeDtypeStruct((subs * SUBDIM, K), F32),
            jax.ShapeDtypeStruct((block, width), F32),
        ),
        in_specs=[pl.BlockSpec(memory_space=pl.ANY)] * 4,
        out_specs=(vmem, vmem),
        scratch_shapes=[
            pltpu.VMEM((keys, half), BF16),
            pltpu.VMEM((2 * half, width), BF16),
            pltpu.VMEM((subs, keys), jnp.int32),
            pltpu.VMEM((width, K), F32),
            pltpu.VMEM((keys, half), BF16),
            pltpu.VMEM((rows_count, keys, block), BF16),
            pltpu.VMEM((rows_count, subs, keys), BF16),
            pltpu.VMEM((rows_count, subs, keys), jnp.int32),
            pltpu.VMEM((width, keys), BF16),
            pltpu.VMEM((rows_count, tall, K), F32),
            pltpu.VMEM((outer, tall, K), F32),
            pltpu.VMEM((outer - 1, tall, K), F32),
            pltpu.VMEM((outer - 1, tall, K), F32),
            pltpu.VMEM((width, K), BF16),
            pltpu.VMEM((rows_count, width, keys), BF16),
            pltpu.SemaphoreType.DMA((4,)),
            pltpu.SemaphoreType.DMA((copies,)),
            pltpu.SemaphoreType.DMA((copies,)),
            pltpu.SemaphoreType.DMA((outer,)),
            pltpu.SemaphoreType.DMA((rows_count,)),
            pltpu.SemaphoreType.DMA((rows_count,)),
        ],
        compiler_params=pltpu.CompilerParams(
            collective_id=0, has_side_effects=True, vmem_limit_bytes=48 * 1024 * 1024
        ),
    )(
        states,
        rotation,
        codes.T,
        prior_codebook.transpose(0, 2, 1).reshape(subs * SUBDIM, K),
    )
    return book_t.reshape(subs, SUBDIM, K).transpose(0, 2, 1), cross


def pick(mesh):
    rows_count = mesh.shape["row"]

    def run(states, rotation, codes, prior_codebook):
        fits = (
            rows_count % 2 == 0
            and rows_count <= 16
            and codes.shape[1] % rows_count == 0
            and (codes.shape[1] // rows_count * 2) % 8 == 0
            and rotation.shape[0] % (16 * rows_count) == 0
        )
        if not fits:
            return shards(states, rotation, codes, prior_codebook)
        return fused(rows_count, states, rotation, codes, prior_codebook)

    return run


def solution(mesh):
    placed = (
        P(("slab", "row"), "sub"),
        P(None, "sub"),
        P(("slab", "row"), "sub"),
        P(("slab", "sub"), None, None),
    )
    return jax.shard_map(
        pick(mesh),
        mesh=mesh,
        in_specs=placed,
        out_specs=(P(("slab", "sub"), None, None), P(("slab", "row"), "sub")),
        check_vma=False,
    )
```

```python
import functools
import math

import jax
import jax.numpy as jnp
from jax import lax
from jax.experimental import pallas as pl
from jax.experimental.pallas import tpu as pltpu
from jax.sharding import PartitionSpec as P

SUBDIM = 16
K = 256


def shards(states, rotation, codes, prior_codebook):
    row_keys = states.shape[0]
    local_subs = codes.shape[1]
    local_width = rotation.shape[1]
    rows_count = lax.axis_size("row")
    labels = jnp.arange(K, dtype=jnp.int32)
    full_states = lax.all_gather(states, "sub", axis=1, tiled=True)
    rotated = jnp.dot(full_states, rotation, preferred_element_type=jnp.float32).astype(
        jnp.bfloat16
    )
    owned = local_width // rows_count
    repeat = max(1, SUBDIM // owned)
    owned_codes = max(1, owned // SUBDIM)
    piece_width = owned // owned_codes
    spread_codes = jnp.repeat(codes, repeat, axis=1)
    moved_rows, moved_codes = (
        lax.all_to_all(rotated, "row", split_axis=1, concat_axis=0, tiled=True),
        lax.all_to_all(spread_codes, "row", split_axis=1, concat_axis=0, tiled=True),
    )
    all_keys = moved_rows.shape[0]
    block_rows = math.gcd(all_keys, 4096)
    block_count = all_keys // block_rows
    rows_blocks = moved_rows.reshape(block_count, block_rows, owned)
    codes_blocks = moved_codes.reshape(block_count, block_rows, moved_codes.shape[1])

    def add_block(carry, pair):
        total_sum, total_count = carry
        row_block, code_block = pair
        new_sums = []
        new_counts = []
        for which in range(owned_codes):
            onehot = (code_block[:, which][:, None] == labels[None, :]).astype(jnp.bfloat16)
            piece = row_block[:, which * piece_width : (which + 1) * piece_width]
            new_sums.append(
                lax.dot_general(
                    onehot, piece, (((0,), (0,)), ((), ())), preferred_element_type=jnp.float32
                )
            )
            new_counts.append(jnp.sum(onehot, axis=0, dtype=jnp.float32))
        return ((total_sum + jnp.stack(new_sums), total_count + jnp.stack(new_counts)), None)

    start_sum = jnp.zeros((owned_codes, K, piece_width), jnp.float32)
    start_count = jnp.zeros((owned_codes, K), jnp.float32)
    (owner_sum, owner_count), _ = lax.scan(
        add_block, (start_sum, start_count), (rows_blocks, codes_blocks)
    )
    every_sum, every_count = (
        lax.all_gather(owner_sum, "row", axis=0, tiled=True),
        lax.all_gather(owner_count, "row", axis=0, tiled=True),
    )
    pieces = SUBDIM // piece_width
    sums = (
        every_sum.reshape(local_subs, pieces, K, piece_width)
        .transpose(0, 2, 1, 3)
        .reshape(local_subs, K, SUBDIM)
    )
    counts = every_count.reshape(local_subs, pieces, K)[:, 0, :]
    codebook = (sums + prior_codebook) / (counts[:, :, None] + 1.0)
    small_book = codebook.astype(jnp.bfloat16)
    group_size = math.gcd(8, local_subs)
    group_count = local_subs // group_size
    book_groups = small_book.reshape(group_count, group_size, K, SUBDIM)
    code_groups = codes.T.reshape(group_count, group_size, row_keys)

    def lookup_group(pair):
        book_part, code_part = pair
        onehot = (code_part[:, :, None] == labels[None, None, :]).astype(jnp.bfloat16)
        found = lax.dot_general(
            onehot, book_part, (((2,), (1,)), ((0,), (0,))), preferred_element_type=jnp.float32
        )
        return found.astype(jnp.bfloat16)

    looked = lax.map(lookup_group, (book_groups, code_groups))
    rebuilt = (
        looked.reshape(local_subs, row_keys, SUBDIM)
        .transpose(1, 0, 2)
        .reshape(row_keys, local_width)
    )
    cross = lax.psum_scatter(
        lax.dot_general(
            full_states, rebuilt, (((0,), (0,)), ((), ())), preferred_element_type=jnp.float32
        ),
        "row",
        scatter_dimension=0,
        tiled=True,
    )
    return (codebook, cross)


MESH = pl.DeviceIdType.MESH
BF16 = jnp.bfloat16
F32 = jnp.float32
NT = (((1,), (1,)), ((), ()))


LANES = 128


def pick_lanes(table, at):
    return jnp.take_along_axis(table, at, axis=1, mode="promise_in_bounds")


def kernel(
    rows_count,
    states_ref,
    rotation_ref,
    codes_ref,
    prior_ref,
    book_ref,
    cross_ref,
    states_v,
    rotation_v,
    codes_v,
    prior_v,
    other,
    all_states,
    all_codes,
    codes_i,
    rotated_t,
    part,
    pair_sum,
    line_out,
    line_sum,
    small_book,
    rebuilt_t,
    local_sem,
    send_sem,
    recv_sem,
    out_sem,
    pass_sem,
    block_sem,
):
    outer = rows_count // 2
    me = lax.axis_index("row")
    sub = lax.axis_index("sub")
    deep, side = me // 2, me % 2
    mate = deep * 2 + 1 - side
    keys, half = states_v.shape
    subs = codes_v.shape[0]
    owned = subs // rows_count
    feats = owned * SUBDIM
    block = cross_ref.shape[0]
    per_half = rows_count // 2
    primary = me // per_half == sub
    hops = sorted(range(outer), key=lambda k: (k == 0, -min(k, outer - k)))
    order = [k for k in reversed(hops) if k != 0]
    used = []

    def copy(src, dst, where):
        index = len(used)
        made = pltpu.make_async_remote_copy(
            src_ref=src,
            dst_ref=dst,
            send_sem=send_sem.at[index],
            recv_sem=recv_sem.at[index],
            device_id=where,
            device_id_type=MESH,
        )
        made.start()
        used.append(made)
        return made

    def line(k):
        return lax.rem(deep + k, outer)

    def back(k):
        return lax.rem(deep + outer - k, outer)

    loads = []
    for index, (src, dst) in enumerate(
        (
            (states_ref, states_v),
            (codes_ref, codes_v),
            (rotation_ref, rotation_v),
            (prior_ref, prior_v),
        )
    ):
        loads.append(pltpu.make_async_copy(src, dst, local_sem.at[index]))
        loads[-1].start()

    barrier = pltpu.get_barrier_semaphore()
    pl.semaphore_signal(barrier, inc=1, device_id={"sub": 1 - sub}, device_id_type=MESH)
    for k in range(1, rows_count):
        pl.semaphore_signal(
            barrier, inc=1, device_id={"row": lax.rem(me + k, rows_count)}, device_id_type=MESH
        )
    pl.semaphore_wait(barrier, rows_count)

    loads[0].wait()
    swap = copy(states_v, other, {"sub": 1 - sub})

    def columns(q):
        return states_v.at[:, pl.ds(pl.multiple_of(q * block, block), block)]

    def give(q):
        owner = sub * per_half + q
        return pltpu.make_async_remote_copy(
            src_ref=columns(q),
            dst_ref=all_states.at[me],
            send_sem=out_sem.at[q],
            recv_sem=block_sem.at[me],
            device_id={"row": owner},
            device_id_type=MESH,
        )

    def forward(source):
        return pltpu.make_async_remote_copy(
            src_ref=all_states.at[source],
            dst_ref=all_states.at[source],
            send_sem=pass_sem.at[source],
            recv_sem=block_sem.at[source],
            device_id={"sub": 1 - sub},
            device_id_type=MESH,
        )

    loads[1].wait()
    all_codes[me] = codes_v[...].astype(F32).astype(BF16)
    codes_along = {}
    for k in hops:
        if k != 0:
            codes_along[k] = copy(
                all_codes.at[me], all_codes.at[me], {"row": line(k) * 2 + side}
            )
    codes_across = {0: copy(all_codes.at[me], all_codes.at[me], {"row": mate})}
    for turn in range(per_half):
        q = lax.rem(me + turn, per_half)

        @pl.when(sub * per_half + q != me)
        def _():
            give(q).start()

    @pl.when(primary)
    def _():
        all_states[me] = columns(lax.rem(me, per_half))[...]
        forward(me).start()

    loads[2].wait()
    total = jnp.dot(
        states_v[...],
        rotation_v[pl.ds(pl.multiple_of(sub * half, half), half), :],
        preferred_element_type=F32,
    )
    swap.wait_recv()
    total = total + jnp.dot(
        other[...],
        rotation_v[pl.ds(pl.multiple_of((1 - sub) * half, half), half), :],
        preferred_element_type=F32,
    )
    rotated_t[...] = total.astype(BF16).T

    labels = lax.broadcasted_iota(jnp.int32, (K, keys), 0)
    ones = jnp.ones((SUBDIM, keys), BF16)

    def sum_block(owner):
        for j in range(owned):
            m = owner * owned + j
            row = codes_v[pl.ds(m, 1), :]
            hot = jnp.where(row == labels, 1.0, 0.0).astype(BF16)
            piece = rotated_t[pl.ds(pl.multiple_of(m * SUBDIM, SUBDIM), SUBDIM), :]
            found = lax.dot_general(
                jnp.concatenate([piece, ones], axis=0), hot, NT, preferred_element_type=F32
            )
            part[owner, j * SUBDIM : (j + 1) * SUBDIM, :] = found[:SUBDIM]
            part[owner, feats + 2 * j : feats + 2 * j + 2, :] = found[SUBDIM : SUBDIM + 2]

    pair = {}
    for k in hops:
        owner = line(k) * 2 + 1 - side
        sum_block(owner)
        pair[k] = copy(part.at[owner], pair_sum.at[k], {"row": mate})
    for k in hops:
        sum_block(line(k) * 2 + side)
    lines = {}
    mine = None
    for k in hops:
        pair[k].wait_recv()
        both = part[line(k) * 2 + side] + pair_sum[k]
        if k == 0:
            mine = both
        else:
            line_out[k - 1] = both
            lines[k] = copy(
                line_out.at[k - 1], line_sum.at[k - 1], {"row": line(k) * 2 + side}
            )
    for k in order:
        codes_along[k].wait_recv()
        source = back(k) * 2 + side
        codes_across[k] = copy(all_codes.at[source], all_codes.at[source], {"row": mate})
    loads[3].wait()
    for k in hops:
        if k != 0:
            lines[k].wait_recv()
            mine = mine + line_sum[k - 1]
    for j in range(owned):
        own_rows = pl.ds(pl.multiple_of(me * feats, feats) + j * SUBDIM, SUBDIM)
        fitted = (mine[j * SUBDIM : (j + 1) * SUBDIM] + prior_v[own_rows, :]) / (
            mine[feats + 2 * j : feats + 2 * j + 1] + 1.0
        )
        small_book[own_rows, :] = fitted.astype(BF16)

    def book_rows(owner):
        return small_book.at[pl.ds(pl.multiple_of(owner * feats, feats), feats), :]

    along = {}
    for k in hops:
        if k != 0:
            along[k] = copy(book_rows(me), book_rows(me), {"row": line(k) * 2 + side})
    across = {0: copy(book_rows(me), book_rows(me), {"row": mate})}

    for k in range(1, rows_count):
        source = lax.rem(me + k, rows_count)
        forward(source).wait_recv()

        @pl.when(primary)
        def _():
            forward(source).start()

    for k in order:
        codes_across[k].wait_recv()
    codes_across[0].wait_recv()

    def look_up(owner):
        base = pl.multiple_of(owner * owned, owned)
        spans = [
            pl.ds(pl.multiple_of((base + j) * SUBDIM, SUBDIM), SUBDIM) for j in range(owned)
        ]
        for rows in spans:
            book_ref[rows, :] = small_book[rows, :].astype(F32)

        @pl.loop(0, rows_count, unroll=8)
        def _(source):
            for j, rows in enumerate(spans):
                row = codes_i[source, pl.ds(base + j, 1), :]
                for c in range(keys // LANES):
                    code = jnp.broadcast_to(row[:, c * LANES : (c + 1) * LANES], (8, LANES))
                    upper = code >= LANES
                    at = jnp.where(upper, code - LANES, code)
                    found = []
                    for h in range(SUBDIM // 8):
                        part_rows = pl.ds(pl.multiple_of((base + j) * SUBDIM, SUBDIM) + 8 * h, 8)
                        low = book_ref[part_rows, :LANES]
                        high = book_ref[part_rows, LANES:]
                        found.append(jnp.where(upper, pick_lanes(high, at), pick_lanes(low, at)))
                    rebuilt_t[source, rows, c * LANES : (c + 1) * LANES] = jnp.concatenate(
                        found, axis=0
                    ).astype(BF16)

    for source in range(rows_count):
        codes_i[source] = all_codes[source].astype(F32).astype(jnp.int32)
    look_up(me)
    for k in order:
        along[k].wait_recv()
        source = back(k) * 2 + side
        across[k] = copy(book_rows(source), book_rows(source), {"row": mate})
    for k in order:
        look_up(back(k) * 2 + side)
    across[0].wait_recv()
    look_up(mate)
    for k in order:
        across[k].wait_recv()
        look_up(back(k) * 2 + 1 - side)

    @pl.when(jnp.logical_not(primary))
    def _():
        forward(me).wait_recv()

    total = jnp.zeros(cross_ref.shape, F32)
    for source in range(rows_count):
        total = total + lax.dot_general(
            all_states[source].T, rebuilt_t[source], NT, preferred_element_type=F32
        )
    cross_ref[...] = total

    for q in range(per_half):

        @pl.when(sub * per_half + q != me)
        def _():
            give(q).wait_send()

    @pl.when(primary)
    def _():
        for source in range(rows_count):
            forward(source).wait_send()

    for made in used:
        made.wait_send()


def fused(rows_count, states, rotation, codes, prior_codebook):
    keys, half = states.shape
    width = rotation.shape[1]
    subs = codes.shape[1]
    outer = rows_count // 2
    feats = subs // rows_count * SUBDIM
    tall = feats + 2 * (subs // rows_count)
    block = rotation.shape[0] // rows_count
    copies = 7 * outer
    vmem = pl.BlockSpec(memory_space=pltpu.VMEM)
    book_t, cross = pl.pallas_call(
        functools.partial(kernel, rows_count),
        out_shape=(
            jax.ShapeDtypeStruct((subs * SUBDIM, K), F32),
            jax.ShapeDtypeStruct((block, width), F32),
        ),
        in_specs=[pl.BlockSpec(memory_space=pl.ANY)] * 4,
        out_specs=(vmem, vmem),
        scratch_shapes=[
            pltpu.VMEM((keys, half), BF16),
            pltpu.VMEM((2 * half, width), BF16),
            pltpu.VMEM((subs, keys), jnp.int32),
            pltpu.VMEM((width, K), F32),
            pltpu.VMEM((keys, half), BF16),
            pltpu.VMEM((rows_count, keys, block), BF16),
            pltpu.VMEM((rows_count, subs, keys), BF16),
            pltpu.VMEM((rows_count, subs, keys), jnp.int32),
            pltpu.VMEM((width, keys), BF16),
            pltpu.VMEM((rows_count, tall, K), F32),
            pltpu.VMEM((outer, tall, K), F32),
            pltpu.VMEM((outer - 1, tall, K), F32),
            pltpu.VMEM((outer - 1, tall, K), F32),
            pltpu.VMEM((width, K), BF16),
            pltpu.VMEM((rows_count, width, keys), BF16),
            pltpu.SemaphoreType.DMA((4,)),
            pltpu.SemaphoreType.DMA((copies,)),
            pltpu.SemaphoreType.DMA((copies,)),
            pltpu.SemaphoreType.DMA((outer,)),
            pltpu.SemaphoreType.DMA((rows_count,)),
            pltpu.SemaphoreType.DMA((rows_count,)),
        ],
        compiler_params=pltpu.CompilerParams(
            collective_id=0, has_side_effects=True, vmem_limit_bytes=48 * 1024 * 1024
        ),
    )(
        states,
        rotation,
        codes.T,
        prior_codebook.transpose(0, 2, 1).reshape(subs * SUBDIM, K),
    )
    return book_t.reshape(subs, SUBDIM, K).transpose(0, 2, 1), cross


def pick(mesh):
    rows_count = mesh.shape["row"]

    def run(states, rotation, codes, prior_codebook):
        fits = (
            rows_count % 2 == 0
            and rows_count <= 16
            and codes.shape[1] % rows_count == 0
            and (codes.shape[1] // rows_count * 2) % 8 == 0
            and rotation.shape[0] % (16 * rows_count) == 0
        )
        if not fits:
            return shards(states, rotation, codes, prior_codebook)
        return fused(rows_count, states, rotation, codes, prior_codebook)

    return run


def solution(mesh):
    placed = (
        P(("slab", "row"), "sub"),
        P(None, "sub"),
        P(("slab", "row"), "sub"),
        P(("slab", "sub"), None, None),
    )
    return jax.shard_map(
        pick(mesh),
        mesh=mesh,
        in_specs=placed,
        out_specs=(P(("slab", "sub"), None, None), P(("slab", "row"), "sub")),
        check_vma=False,
    )
```
